32 devices in a mesh: comp: 8 (over z, core), feat: 4 (over y, x).
Axes of the slice: x: 2, y: 2, z: 4, core: 2. Of those that a mesh axis runs over, the one named last changes fastest.
Arguments:
- block_values: bfloat16 [8, 4, 24, 128, 128], P('comp', 'feat'), may hold values from -0.125 to 0.125
- block_rows: int32 [8, 4, 24], P('comp', 'feat'), may hold values from 0 to 15, as said below
- block_cols: int32 [8, 4, 24], P('comp', 'feat'), may hold values from 0 to 13, as said below
- block_counts: int32 [8, 4], P('comp', 'feat'), may hold values from 8 to 24, as said below
- right_side: float32 [16384, 128], P(('comp', 'feat')), may hold values from -6 to 6
- ridge: float32 [128], replicated, may hold values from 0.1 to 2
Outputs:
- solution: float32 [7168, 128], P('feat')
- residual: float32 [16384, 128], P(('comp', 'feat'))
The draws below stay inside these ranges and needn't reach their ends.
Inputs may be any that keep to these rules, and one draw needn't show every extreme that they name: Within one device the listed (block_rows, block_cols) pairs of all 24 slots are distinct; block rows are very uneven in how many blocks they hold. `block_cols`: see block_rows. `block_counts`: slots at or beyond a device's count are ignored; some device is full in every draw.
All inputs are finite; a program needn't handle non-finite values.
Results may differ from the reference program's by a relative error of at most 0.0029.
Values may be sent and summed in bfloat16 or wider, within the bound.
A program may use at most 64 MiB of HBM per device.

```python
import math
import jax
import jax.numpy as jnp
from jax import lax

BLOCK = 128
RESP = 128
RB_DEV = 16
CB_DEV = 14
BLK_DEV = 24
ITERS = 2
COMPS = 16384
FEATS = 7168
N_COMP = 8
N_FEAT = 4


def coordinate_table(key):
    heavy_key = jax.random.fold_in(key, 11)
    noise_key = jax.random.fold_in(key, 12)
    positions = RB_DEV * CB_DEV
    heavy = jax.random.randint(heavy_key, (N_COMP, N_FEAT, RB_DEV), 0, 4)
    noise = jax.random.randint(noise_key, (N_COMP, N_FEAT, positions), 0, 1000)
    row_of = jnp.arange(positions) // CB_DEV
    score = (jnp.take(heavy, row_of, axis=2) * 1000 + noise) * positions + jnp.arange(positions)
    _, order = lax.top_k(score, BLK_DEV)
    return ((order // CB_DEV).astype(jnp.int32), (order % CB_DEV).astype(jnp.int32))


def draw_block_rows(key, part):
    return coordinate_table(key)[0]


def draw_block_cols(key, part):
    return coordinate_table(key)[1]


def draw_block_counts(key, part):
    base = jax.random.randint(jax.random.fold_in(key, 21), (N_COMP * N_FEAT,), max(1, BLK_DEV // 3), BLK_DEV + 1)
    chosen = jax.random.randint(jax.random.fold_in(key, 22), (), 0, N_COMP * N_FEAT)
    full = jnp.where(jnp.arange(N_COMP * N_FEAT) == chosen, BLK_DEV, base)
    return full.reshape(N_COMP, N_FEAT).astype(jnp.int32)


def steps_of(stream_key, shape, split, smallest, largest):
    factor_of, own = 1.0, jax.random.fold_in(stream_key, 6)
    for axis_at, shards_of in split:
        heights = jnp.exp(jax.random.uniform(jax.random.fold_in(own, axis_at), (shards_of,), jnp.float32, smallest / len(split), largest / len(split)))
        factor_of = factor_of * jnp.repeat(heights, shape[axis_at] // shards_of).reshape([-1 if axis == axis_at else 1 for axis in range(len(shape))])
    return factor_of


def scatter_about(rng, extent, width, reach, shards=(), kind=jnp.bfloat16):
    array = jax.random.normal(rng, extent, jnp.float32) * width
    if len(shards) > 0:
        array = steps_of(rng, extent, shards, -0.22, 0.18) * array
    return jnp.clip(array, min=-reach, max=reach).astype(kind)


def setup_inputs(seed: int = 0) -> dict:
    keys = jax.random.split(jax.random.key(seed), 7)
    return {
        "block_values": scatter_about(keys[0], (N_COMP, N_FEAT, BLK_DEV, BLOCK, BLOCK), (BLOCK * BLK_DEV * N_COMP // CB_DEV) ** -0.5, 0.125, ((0, 8), (1, 4))),
        "block_rows": draw_block_rows(jax.random.fold_in(keys[6], 71), 0),
        "block_cols": draw_block_cols(jax.random.fold_in(keys[6], 71), 0),
        "block_counts": draw_block_counts(jax.random.fold_in(keys[6], 71), 0),
        "right_side": scatter_about(keys[4], (COMPS, RESP), 1.0, 6.0, ((0, 32),), jnp.float32),
        "ridge": jnp.clip(jnp.exp(jax.random.uniform(keys[5], (RESP,), jnp.float32, math.log(0.1), math.log(2.0))), 0.1, 2.0),
    }


def rounded(matrix):
    return lax.optimization_barrier(matrix.astype(jnp.bfloat16))


def reference(block_values, block_rows, block_cols, block_counts, right_side, ridge):
    responses = right_side.shape[1]
    slot_live = (jnp.arange(BLK_DEV)[None, None, :] < block_counts[:, :, None]).astype(jnp.float32)
    feat_index = jnp.arange(N_FEAT)[:, None]

    def forward(low_panel):
        col_panels = low_panel.reshape(N_FEAT, CB_DEV, BLOCK, responses)

        def per_comp(comp_index):
            selected = col_panels[feat_index, block_cols[comp_index]].astype(jnp.float32)
            block_products = jnp.einsum("fsij,fsjk->fsik", block_values[comp_index].astype(jnp.float32), selected)
            row_lookup_table = (block_rows[comp_index][:, :, None] == jnp.arange(RB_DEV)[None, None, :]).astype(jnp.float32)
            row_lookup_table = row_lookup_table * slot_live[comp_index][:, :, None]
            return jnp.einsum("vmt,vmyj->tyj", row_lookup_table, block_products, precision=lax.Precision.HIGHEST)

        return lax.map(per_comp, jnp.arange(N_COMP)).reshape(COMPS, responses)

    def backward(low_slab):
        row_slabs = low_slab.reshape(N_COMP, RB_DEV, BLOCK, responses)

        def per_comp(running_accumulator, comp_index):
            selected = row_slabs[comp_index][block_rows[comp_index]].astype(jnp.float32)
            block_products = jnp.einsum("fsij,fsik->fsjk", block_values[comp_index].astype(jnp.float32), selected)
            col_table = (block_cols[comp_index][:, :, None] == jnp.arange(CB_DEV)[None, None, :]).astype(jnp.float32)
            col_table = col_table * slot_live[comp_index][:, :, None]
            added = jnp.einsum("fsq,fsjk->fqjk", col_table, block_products, precision=lax.Precision.HIGHEST)
            return running_accumulator + added, 0

        start = jnp.zeros((N_FEAT, CB_DEV, BLOCK, responses), jnp.float32)
        total, _ = lax.scan(per_comp, start, jnp.arange(N_COMP))
        return total.reshape(FEATS, responses)

    residual = right_side
    solution = jnp.zeros((FEATS, responses), jnp.float32)
    gradient = backward(rounded(residual))
    energy = jnp.sum(gradient * gradient, axis=0)
    search_direction = gradient
    for step_index in range(ITERS):
        image_rows = forward(rounded(search_direction))
        curvature = jnp.sum(image_rows * image_rows, axis=0) + ridge * jnp.sum(search_direction * search_direction, axis=0)
        step_size = energy / curvature
        solution = solution + step_size * search_direction
        residual = residual - step_size * image_rows
        if step_index + 1 < ITERS:
            gradient = backward(rounded(residual)) - ridge * solution
            next_energy = jnp.sum(gradient * gradient, axis=0)
            search_direction = gradient + (next_energy / energy) * search_direction
            energy = next_energy
    return solution, residual
```

```python
import functools

import jax
import jax.numpy as jnp
from jax import lax
from jax.experimental import pallas as pl
from jax.experimental.pallas import tpu as pltpu
from jax.sharding import PartitionSpec as P

CB_DEV = 14
MESH = pl.DeviceIdType.MESH
F32 = jnp.float32
BF16 = jnp.bfloat16


def kernel(
    nz, nf, slots, rb, edge, sr,
    rows, cols, count, values, rs, ridge, sol_out, res_out,
    vt, run, slab_a, slab_b, part, sib, pair, zbuf, dirs, panels, img, rbuf, g_f32, i_f32,
    link, sc_src, sc_feat, sc_mid, sc_comp, send_sems, recv_sems,
):
    comp, feat = lax.axis_index("comp"), lax.axis_index("feat")
    core, z = lax.rem(comp, 2), comp // 2
    half = CB_DEV // 2 * edge
    hp = nz * sr
    own_blocks = rb // nf
    sibling = {"comp": comp + 1 - 2 * core}
    n_comp = 2 * nz
    pending = []
    used = [0]

    def zpeer(k):
        return {"comp": lax.rem(z + k, nz) * 2 + core}

    def fpeer(k):
        return {"feat": lax.rem(feat + k, nf)}

    def cpeer(k):
        return {"comp": lax.rem(comp + k, n_comp)}

    def send(src, dst, device):
        at = used[0]
        used[0] += 1
        copy = pltpu.make_async_remote_copy(
            src_ref=src,
            dst_ref=dst,
            send_sem=send_sems.at[at],
            recv_sem=recv_sems.at[at],
            device_id=device,
            device_id_type=MESH,
        )
        copy.start()
        pending.append(copy)
        return copy

    def shard(k):
        return pl.multiple_of(lax.rem(z + k, nz) * sr, 16)

    slabs = (slab_a, slab_b)
    prev_c, last_c = 0, slots
    prev_r, last_r = slots + CB_DEV, 2 * slots + CB_DEV

    def last_slot(keys, wanted, limit):
        found = jnp.int32(slots)
        for t in range(slots):
            found = jnp.where((keys[t] == wanted) & (t < limit), t, found)
        return found

    def make_links(keys, groups, prev, last):
        @pl.loop(0, slots)
        def _(s):
            link[prev + s] = last_slot(keys, keys[s], s)

        live = count[0]

        @pl.loop(0, groups)
        def _(q):
            link[last + q] = last_slot(keys, q, live)

    barrier = pltpu.get_barrier_semaphore()
    for k in range(1, n_comp):
        pl.semaphore_signal(barrier, inc=1, device_id=cpeer(k), device_id_type=MESH)
    for k in range(1, nf):
        pl.semaphore_signal(barrier, inc=1, device_id=fpeer(k), device_id_type=MESH)
    mine = pl.ds(feat * own_blocks, own_blocks)
    slab_a[mine] = rs[...].astype(BF16).reshape(own_blocks, edge, edge)
    pl.semaphore_wait(barrier, n_comp - 1 + nf - 1)

    def gather_feat(which):
        return [
            send(slabs[which].at[mine], slabs[which].at[mine], fpeer(k)) for k in range(1, nf)
        ]

    def backward(which):
        for s in range(slots):
            product = jnp.dot(vt[s], slabs[which][rows[s]], preferred_element_type=F32)
            run[s] = product + run[link[prev_c + s]]
        for q in range(CB_DEV):
            h, p = q // (CB_DEV // 2), q % (CB_DEV // 2)
            part[which, pl.ds(h * hp + p * edge, edge)] = run[link[last_c + q]]
        if hp > half:
            for h in range(2):
                part[which, pl.ds(h * hp + half, hp - half)] = jnp.zeros((hp - half, edge), F32)

    def scatter_comp(which):
        order = list(range(1, nz)) + [0]
        halves = {}
        for k in order:
            theirs = pl.multiple_of((1 - core) * hp + shard(k), 16)
            halves[k] = send(
                part.at[which, pl.ds(theirs, sr)], sib.at[which, pl.ds(shard(k), sr)], sibling
            )
        total = None
        arrivals = []
        for k in order:
            halves[k].wait_recv()
            ours = pl.multiple_of(core * hp + shard(k), 16)
            both = part[which, pl.ds(ours, sr)] + sib[which, pl.ds(shard(k), sr)]
            if k:
                pair[which, k] = both.astype(BF16)
                arrivals.append(send(pair.at[which, k], zbuf.at[which, k], zpeer(k)))
            else:
                total = both
        for k, copy in zip(order, arrivals):
            copy.wait_recv()
            total = total + zbuf[which, k].astype(F32)
        return total

    def gather_comp(which, piece):
        here = pl.ds(pl.multiple_of(core * hp + shard(0), 16), sr)
        dirs[which, here] = piece.astype(BF16)
        across = [send(dirs.at[which, here], dirs.at[which, here], zpeer(k)) for k in range(1, nz)]
        beside = [send(dirs.at[which, here], dirs.at[which, here], sibling)]
        for k, copy in zip(range(1, nz), across):
            copy.wait_recv()
            came = pl.ds(pl.multiple_of(core * hp + shard(nz - k), 16), sr)
            beside.append(send(dirs.at[which, came], dirs.at[which, came], sibling))
        for copy in beside:
            copy.wait_recv()

    def forward(which):
        for q in range(CB_DEV):
            h, p = q // (CB_DEV // 2), q % (CB_DEV // 2)
            panels[q] = dirs[which, pl.ds(h * hp + p * edge, edge)]
        for s in range(slots):
            product = jnp.dot(values[s], panels[cols[s]], preferred_element_type=F32)
            run[s] = product + run[link[prev_r + s]]
        for r in range(rb):
            img[which, r] = run[link[last_r + r]].astype(BF16)

    def scatter_feat(which):
        copies = [
            send(
                img.at[which, pl.ds(lax.rem(feat + k, nf) * own_blocks, own_blocks)],
                rbuf.at[which, k],
                fpeer(k),
            )
            for k in range(1, nf)
        ]
        total = img[which, mine].astype(F32)
        for k, copy in zip(range(1, nf), copies):
            copy.wait_recv()
            total = total + rbuf[which, k].astype(F32)
        return total.reshape(own_blocks * edge, edge)

    def column_sum(x):
        return jnp.sum(x, axis=0, keepdims=True)

    def sums_out(which, rows):
        for i, row in enumerate(rows):
            sc_src[which, pl.ds(i, 1)] = row
        return [send(sc_src.at[which], sc_feat.at[which, k], fpeer(k)) for k in range(1, nf)]

    def sums_on(which, copies):
        total = sc_src[which]
        for k, copy in zip(range(1, nf), copies):
            copy.wait_recv()
            total = total + sc_feat[which, k]
        sc_mid[which] = total
        return [send(sc_mid.at[which], sc_comp.at[which, k], cpeer(k)) for k in range(1, n_comp)]

    def sums_in(which, copies):
        total = sc_mid[which]
        for k, copy in zip(range(1, n_comp), copies):
            copy.wait_recv()
            total = total + sc_comp[which, k]
        return total

    sc_src[...] = jnp.zeros_like(sc_src)
    copies = gather_feat(0)
    run[slots] = jnp.zeros((edge, edge), F32)
    for s in range(slots):
        vt[s] = values[s].T
    make_links(cols, CB_DEV, prev_c, last_c)
    make_links(rows, rb, prev_r, last_r)
    for copy in copies:
        copy.wait_recv()
    backward(0)
    g0 = scatter_comp(0)
    g_f32[...] = g0
    gather_comp(0, g0)
    forward(0)
    i0 = scatter_feat(0)
    i_f32[...] = i0
    g0 = g_f32[...]
    sums = sums_out(0, [column_sum(i0 * i0), column_sum(g0 * g0)])
    first = sums_in(0, sums_on(0, sums))
    penalty = ridge[...]
    image0, energy0 = first[0:1], first[1:2]
    step0 = energy0 / (image0 + penalty * energy0)
    i0 = i_f32[...]
    slab_b[mine] = (rs[...] - step0 * i0).astype(BF16).reshape(own_blocks, edge, edge)
    copies = gather_feat(1)
    for copy in copies:
        copy.wait_recv()
    backward(1)
    g1 = scatter_comp(1)
    g0 = g_f32[...]
    g1 = g1 - penalty * (step0 * g0)
    gather_comp(1, g1)
    energy_row, mixed_row = column_sum(g1 * g1), column_sum(g1 * g0)
    forward(1)
    u = scatter_feat(1)
    i0 = i_f32[...]
    sums = sums_out(1, [column_sum(u * u), column_sum(u * i0), energy_row, mixed_row])
    last = sums_in(1, sums_on(1, sums))
    uu, ui, energy1, gg = last[0:1], last[1:2], last[2:3], last[3:4]
    beta = energy1 / energy0
    curvature = (
        uu + beta * (2.0 * ui + beta * image0)
        + penalty * (energy1 + beta * (2.0 * gg + beta * energy0))
    )
    step1 = energy1 / curvature
    weight = step0 + step1 * beta
    res_out[...] = rs[...] - weight * i0 - step1 * u
    for h in range(2):
        take = pl.ds(h * hp, half)
        sol_out[pl.ds(h * half, half)] = weight * dirs[0, take].astype(F32) + step1 * dirs[
            1, take
        ].astype(F32)
    for copy in pending:
        copy.wait_send()


def shards(nz, nf, block_values, block_rows, block_cols, block_counts, right_side, ridge):
    values = block_values[0, 0]
    rows, cols, count = block_rows[0, 0], block_cols[0, 0], block_counts[0]
    slots, edge = values.shape[0], values.shape[1]
    held = right_side.shape[0]
    rb = held * nf // edge
    half = CB_DEV // 2 * edge
    sr = -(-half // (nz * 16)) * 16
    hp = nz * sr
    own = rb // nf
    n_copies = 2 * (2 * (nf - 1) + 2 * (nz - 1) + 2 * nz + (nf - 1) + (2 * nz - 1))
    smem = pl.BlockSpec(memory_space=pltpu.SMEM)
    vmem = pl.BlockSpec(memory_space=pltpu.VMEM)
    return pl.pallas_call(
        functools.partial(kernel, nz, nf, slots, rb, edge, sr),
        out_shape=(
            jax.ShapeDtypeStruct((CB_DEV * edge, edge), F32),
            jax.ShapeDtypeStruct((held, edge), F32),
        ),
        in_specs=[smem, smem, smem, vmem, vmem, vmem],
        out_specs=(vmem, vmem),
        scratch_shapes=[
            pltpu.VMEM((slots, edge, edge), BF16),
            pltpu.VMEM((slots + 1, edge, edge), F32),
            pltpu.VMEM((rb, edge, edge), BF16),
            pltpu.VMEM((rb, edge, edge), BF16),
            pltpu.VMEM((2, 2 * hp, edge), F32),
            pltpu.VMEM((2, hp, edge), F32),
            pltpu.VMEM((2, nz, sr, edge), BF16),
            pltpu.VMEM((2, nz, sr, edge), BF16),
            pltpu.VMEM((2, 2 * hp, edge), BF16),
            pltpu.VMEM((CB_DEV, edge, edge), BF16),
            pltpu.VMEM((2, rb, edge, edge), BF16),
            pltpu.VMEM((2, nf, own, edge, edge), BF16),
            pltpu.VMEM((sr, edge), F32),
            pltpu.VMEM((held, edge), F32),
            pltpu.SMEM((2 * slots + CB_DEV + rb,), jnp.int32),
            pltpu.VMEM((2, 8, edge), F32),
            pltpu.VMEM((2, nf, 8, edge), F32),
            pltpu.VMEM((2, 8, edge), F32),
            pltpu.VMEM((2, 2 * nz, 8, edge), F32),
            pltpu.SemaphoreType.DMA((n_copies,)),
            pltpu.SemaphoreType.DMA((n_copies,)),
        ],
        compiler_params=pltpu.CompilerParams(
            collective_id=0, has_side_effects=True, vmem_limit_bytes=48 * 1024 * 1024
        ),
        cost_estimate=pl.CostEstimate(
            flops=8 * slots * edge**3, bytes_accessed=4 * 1024 * 1024, transcendentals=0
        ),
    )(rows, cols, count, values, right_side, ridge.reshape(1, edge))


def solution(mesh):
    nz, nf = mesh.shape["comp"] // 2, mesh.shape["feat"]
    placed = (
        P("comp", "feat", None, None, None),
        P("comp", "feat", None),
        P("comp", "feat", None),
        P("comp", "feat"),
        P(("comp", "feat"), None),
        P(),
    )
    return jax.shard_map(
        functools.partial(shards, nz, nf),
        mesh=mesh,
        in_specs=placed,
        out_specs=(P("feat", None), P(("comp", "feat"), None)),
        check_vma=False,
    )
```

```python
import functools

import jax
import jax.numpy as jnp
from jax import lax
from jax.experimental import pallas as pl
from jax.experimental.pallas import tpu as pltpu
from jax.sharding import PartitionSpec as P

CB_DEV = 14
MESH = pl.DeviceIdType.MESH
F32 = jnp.float32
BF16 = jnp.bfloat16


def fold(x):
    return x + pltpu.roll(x, x.shape[1] // 2, axis=1)


def kernel(
    nz, nf, slots, rb, edge, sr,
    rows, cols, count, values, rs, ridge, sol_out, res_out,
    vt, run_a, run_b, wide_a, wide_b, slabs, part, sib, pair, zbuf, dirs, img, rbuf,
    r_f32, g_f32, i_f32, link, sc_src, sc_feat, sc_mid, sc_comp, send_sems, recv_sems,
):
    comp, feat = lax.axis_index("comp"), lax.axis_index("feat")
    core, z = lax.rem(comp, 2), comp // 2
    low = edge // 2
    half = CB_DEV // 2 * low
    hp = nz * sr
    own_blocks = rb // nf
    sibling = {"comp": comp + 1 - 2 * core}
    n_comp = 2 * nz
    pending = []
    used = [0]
    mine = pl.ds(feat * own_blocks, own_blocks)

    def zpeer(k):
        return {"comp": lax.rem(z + k, nz) * 2 + core}

    def fpeer(k):
        return {"feat": lax.rem(feat + k, nf)}

    def cpeer(k):
        return {"comp": lax.rem(comp + k, n_comp)}

    def send(src, dst, device):
        at = used[0]
        used[0] += 1
        copy = pltpu.make_async_remote_copy(
            src_ref=src,
            dst_ref=dst,
            send_sem=send_sems.at[at],
            recv_sem=recv_sems.at[at],
            device_id=device,
            device_id_type=MESH,
        )
        copy.start()
        pending.append(copy)
        return copy

    def shard(k):
        return pl.multiple_of(lax.rem(z + k, nz) * sr, 16)

    prev_c, last_c = 0, slots
    prev_r, last_r = slots + CB_DEV, 2 * slots + CB_DEV

    def last_slot(keys, wanted, limit):
        found = jnp.int32(slots)
        for t in range(slots):
            found = jnp.where((keys[t] == wanted) & (t < limit), t, found)
        return found

    def make_links(keys, groups, prev, last):
        @pl.loop(0, slots)
        def _(s):
            link[prev + s] = last_slot(keys, keys[s], s)

        live = count[0]

        @pl.loop(0, groups)
        def _(q):
            link[last + q] = last_slot(keys, q, live)

    left = lax.broadcasted_iota(jnp.int32, (low, edge), 1) < low

    def swap(x):
        return pltpu.roll(x, low, axis=1)

    def widen(wide, at, packed):
        x = packed.astype(F32)
        y = swap(x)
        zero = jnp.zeros_like(x)
        wide[at, pl.ds(0, low)] = jnp.where(left, x, zero).astype(BF16)
        wide[at, pl.ds(low, low)] = jnp.where(left, y, zero).astype(BF16)
        wide[at, pl.ds(2 * low, low)] = jnp.where(left, zero, y).astype(BF16)
        wide[at, pl.ds(3 * low, low)] = jnp.where(left, zero, x).astype(BF16)

    def unpack(x0, x1):
        return jnp.where(left, x0, swap(x1)), jnp.where(left, swap(x0), x1)

    def column_sum(x):
        return jnp.sum(x, axis=0, keepdims=True)

    def stream(h):
        run = (run_a, run_b)[h]
        wide = (wide_a, wide_b)[h]

        def gather_feat(it):
            at = (it, h, mine)
            return [send(slabs.at[at], slabs.at[at], fpeer(k)) for k in range(1, nf)]

        def products(blocks, places, prev):
            for s in range(slots):
                block = jnp.concatenate([blocks[s, :low], blocks[s, low:]], axis=1)
                product = jnp.dot(block, wide[places[s]], preferred_element_type=F32)
                run[s] = product + run[link[prev + s]]

        def backward(it):
            for r in range(rb):
                widen(wide, r, slabs[it, h, r])
            products(vt, rows, prev_c)
            for q in range(CB_DEV):
                d, p = q // (CB_DEV // 2), q % (CB_DEV // 2)
                part[it, h, pl.ds(d * hp + p * low, low)] = run[link[last_c + q]]
            if hp > half:
                for d in range(2):
                    part[it, h, pl.ds(d * hp + half, hp - half)] = jnp.zeros((hp - half, edge), F32)

        def scatter_comp(it):
            order = list(range(1, nz)) + [0]
            halves = {}
            for k in order:
                theirs = pl.multiple_of((1 - core) * hp + shard(k), 16)
                halves[k] = send(
                    part.at[it, h, pl.ds(theirs, sr)], sib.at[it, h, pl.ds(shard(k), sr)], sibling
                )
            yield
            arrivals = []
            total = None
            for k in order:
                halves[k].wait_recv()
                ours = pl.multiple_of(core * hp + shard(k), 16)
                both = part[it, h, pl.ds(ours, sr)] + sib[it, h, pl.ds(shard(k), sr)]
                if k:
                    pair[it, h, k] = both.astype(BF16)
                    arrivals.append(send(pair.at[it, h, k], zbuf.at[it, h, k], zpeer(k)))
                else:
                    total = both
            yield
            for k, copy in zip(order, arrivals):
                copy.wait_recv()
                total = total + zbuf[it, h, k].astype(F32)
            return total

        def gather_comp(it, piece):
            here = (it, h, pl.ds(pl.multiple_of(core * hp + shard(0), 16), sr))
            dirs[here] = piece.astype(BF16)
            across = [send(dirs.at[here], dirs.at[here], zpeer(k)) for k in range(1, nz)]
            beside = [send(dirs.at[here], dirs.at[here], sibling)]
            yield
            for k, copy in zip(range(1, nz), across):
                copy.wait_recv()
                came = (it, h, pl.ds(pl.multiple_of(core * hp + shard(nz - k), 16), sr))
                beside.append(send(dirs.at[came], dirs.at[came], sibling))
            yield
            for copy in beside:
                copy.wait_recv()

        def forward(it):
            for q in range(CB_DEV):
                d, p = q // (CB_DEV // 2), q % (CB_DEV // 2)
                widen(wide, q, dirs[it, h, pl.ds(d * hp + p * low, low)])
            products(values, cols, prev_r)
            for r in range(rb):
                img[it, h, r] = run[link[last_r + r]].astype(BF16)

        def scatter_feat(it):
            copies = [
                send(
                    img.at[it, h, pl.ds(lax.rem(feat + k, nf) * own_blocks, own_blocks)],
                    rbuf.at[it, h, k],
                    fpeer(k),
                )
                for k in range(1, nf)
            ]
            yield
            total = img[it, h, mine].astype(F32)
            for k, copy in zip(range(1, nf), copies):
                copy.wait_recv()
                total = total + rbuf[it, h, k].astype(F32)
            return total.reshape(own_blocks * low, edge)

        def sums(it, parts):
            for i, row in enumerate(parts):
                sc_src[it, h, pl.ds(i, 1)] = row
            copies = [
                send(sc_src.at[it, h], sc_feat.at[it, h, k], fpeer(k)) for k in range(1, nf)
            ]
            yield
            total = sc_src[it, h]
            for k, copy in zip(range(1, nf), copies):
                copy.wait_recv()
                total = total + sc_feat[it, h, k]
            sc_mid[it, h] = total
            copies = [
                send(sc_mid.at[it, h], sc_comp.at[it, h, k], cpeer(k)) for k in range(1, n_comp)
            ]
            yield
            for k, copy in zip(range(1, n_comp), copies):
                copy.wait_recv()
                total = total + sc_comp[it, h, k]
            return fold(total)

        copies = gather_feat(0)
        yield
        for copy in copies:
            copy.wait_recv()
        backward(0)
        g0 = yield from scatter_comp(0)
        g_f32[h] = g0
        yield from gather_comp(0, g0)
        forward(0)
        i0 = yield from scatter_feat(0)
        i_f32[h] = i0
        g0 = g_f32[h]
        first = yield from sums(0, [column_sum(i0 * i0), column_sum(g0 * g0)])
        penalty = ridge[pl.ds(h, 1)]
        image0, energy0 = first[0:1], first[1:2]
        step0 = energy0 / (image0 + penalty * energy0)
        r1 = r_f32[h] - step0 * i_f32[h]
        slabs[1, h, mine] = r1.astype(BF16).reshape(own_blocks, low, edge)
        copies = gather_feat(1)
        yield
        for copy in copies:
            copy.wait_recv()
        backward(1)
        g1 = yield from scatter_comp(1)
        g0 = g_f32[h]
        g1 = g1 - penalty * (step0 * g0)
        energy_row, mixed_row = column_sum(g1 * g1), column_sum(g1 * g0)
        yield from gather_comp(1, g1)
        forward(1)
        u = yield from scatter_feat(1)
        i0 = i_f32[h]
        last = yield from sums(
            1, [column_sum(u * u), column_sum(u * i0), energy_row, mixed_row]
        )
        uu, ui, energy1, gg = last[0:1], last[1:2], last[2:3], last[3:4]
        beta = energy1 / energy0
        curvature = (
            uu + beta * (2.0 * ui + beta * image0)
            + penalty * (energy1 + beta * (2.0 * gg + beta * energy0))
        )
        step1 = energy1 / curvature
        weight = step0 + step1 * beta
        r_f32[h] = r_f32[h] - weight * i_f32[h] - step1 * u
        return weight, step1

    barrier = pltpu.get_barrier_semaphore()
    for k in range(1, n_comp):
        pl.semaphore_signal(barrier, inc=1, device_id=cpeer(k), device_id_type=MESH)
    for k in range(1, nf):
        pl.semaphore_signal(barrier, inc=1, device_id=fpeer(k), device_id_type=MESH)
    for r in range(own_blocks):
        top, bottom = rs[pl.ds(r * edge, low)], rs[pl.ds(r * edge + low, low)]
        for h, x in enumerate(unpack(top, bottom)):
            r_f32[h, pl.ds(r * low, low)] = x
    for h in range(2):
        slabs[0, h, mine] = r_f32[h].astype(BF16).reshape(own_blocks, low, edge)
    sc_src[...] = jnp.zeros_like(sc_src)
    pl.semaphore_wait(barrier, n_comp - 1 + nf - 1)

    streams = [stream(h) for h in range(2)]
    steps = [None, None]
    for g in streams:
        next(g)
    run_a[slots] = jnp.zeros((low, edge), F32)
    run_b[slots] = jnp.zeros((low, edge), F32)
    for s in range(slots):
        vt[s] = values[s].T
    make_links(cols, CB_DEV, prev_c, last_c)
    make_links(rows, rb, prev_r, last_r)
    while None in steps:
        for h, g in enumerate(streams):
            try:
                next(g)
            except StopIteration as done:
                steps[h] = done.value
    for r in range(own_blocks):
        parts = unpack(r_f32[0, pl.ds(r * low, low)], r_f32[1, pl.ds(r * low, low)])
        for d in range(2):
            res_out[pl.ds(r * edge + d * low, low)] = parts[d]
    for q in range(CB_DEV):
        d, p = q // (CB_DEV // 2), q % (CB_DEV // 2)
        take = pl.ds(d * hp + p * low, low)
        found = [
            steps[h][0] * dirs[0, h, take].astype(F32) + steps[h][1] * dirs[1, h, take].astype(F32)
            for h in range(2)
        ]
        parts = unpack(*found)
        for d in range(2):
            sol_out[pl.ds(q * edge + d * low, low)] = parts[d]
    for copy in pending:
        copy.wait_send()


def shards(nz, nf, block_values, block_rows, block_cols, block_counts, right_side, ridge):
    values = block_values[0, 0]
    rows, cols, count = block_rows[0, 0], block_cols[0, 0], block_counts[0]
    slots, edge = values.shape[0], values.shape[1]
    held = right_side.shape[0]
    rb = held * nf // edge
    low = edge // 2
    sr = -(-(CB_DEV // 2 * low) // (nz * 16)) * 16
    hp = nz * sr
    own = rb // nf
    n_copies = 4 * (2 * (nf - 1) + 2 * (nz - 1) + 2 * nz + (nf - 1) + (2 * nz - 1))
    penalties = jnp.tile(ridge.reshape(2, low), (1, 2))
    smem = pl.BlockSpec(memory_space=pltpu.SMEM)
    vmem = pl.BlockSpec(memory_space=pltpu.VMEM)
    return pl.pallas_call(
        functools.partial(kernel, nz, nf, slots, rb, edge, sr),
        out_shape=(
            jax.ShapeDtypeStruct((CB_DEV * edge, edge), F32),
            jax.ShapeDtypeStruct((held, edge), F32),
        ),
        in_specs=[smem, smem, smem, vmem, vmem, vmem],
        out_specs=(vmem, vmem),
        scratch_shapes=[
            pltpu.VMEM((slots, edge, edge), BF16),
            pltpu.VMEM((slots + 1, low, edge), F32),
            pltpu.VMEM((slots + 1, low, edge), F32),
            pltpu.VMEM((max(rb, CB_DEV), 2 * edge, edge), BF16),
            pltpu.VMEM((max(rb, CB_DEV), 2 * edge, edge), BF16),
            pltpu.VMEM((2, 2, rb, low, edge), BF16),
            pltpu.VMEM((2, 2, 2 * hp, edge), F32),
            pltpu.VMEM((2, 2, hp, edge), F32),
            pltpu.VMEM((2, 2, nz, sr, edge), BF16),
            pltpu.VMEM((2, 2, nz, sr, edge), BF16),
            pltpu.VMEM((2, 2, 2 * hp, edge), BF16),
            pltpu.VMEM((2, 2, rb, low, edge), BF16),
            pltpu.VMEM((2, 2, nf, own, low, edge), BF16),
            pltpu.VMEM((2, own * low, edge), F32),
            pltpu.VMEM((2, sr, edge), F32),
            pltpu.VMEM((2, own * low, edge), F32),
            pltpu.SMEM((2 * slots + CB_DEV + rb,), jnp.int32),
            pltpu.VMEM((2, 2, 8, edge), F32),
            pltpu.VMEM((2, 2, nf, 8, edge), F32),
            pltpu.VMEM((2, 2, 8, edge), F32),
            pltpu.VMEM((2, 2, 2 * nz, 8, edge), F32),
            pltpu.SemaphoreType.DMA((n_copies,)),
            pltpu.SemaphoreType.DMA((n_copies,)),
        ],
        compiler_params=pltpu.CompilerParams(
            collective_id=0, has_side_effects=True, vmem_limit_bytes=48 * 1024 * 1024
        ),
        cost_estimate=pl.CostEstimate(
            flops=8 * slots * edge**3, bytes_accessed=4 * 1024 * 1024, transcendentals=0
        ),
    )(rows, cols, count, values, right_side, penalties)


def solution(mesh):
    nz, nf = mesh.shape["comp"] // 2, mesh.shape["feat"]
    placed = (
        P("comp", "feat", None, None, None),
        P("comp", "feat", None),
        P("comp", "feat", None),
        P("comp", "feat"),
        P(("comp", "feat"), None),
        P(),
    )
    return jax.shard_map(
        functools.partial(shards, nz, nf),
        mesh=mesh,
        in_specs=placed,
        out_specs=(P("feat", None), P(("comp", "feat"), None)),
        check_vma=False,
    )
```

```python
import functools

import jax
import jax.numpy as jnp
from jax import lax
from jax.experimental import pallas as pl
from jax.experimental.pallas import tpu as pltpu
from jax.sharding import PartitionSpec as P

CB_DEV = 14
MESH = pl.DeviceIdType.MESH
F32 = jnp.float32
BF16 = jnp.bfloat16


def fold(x):
    return x + pltpu.roll(x, x.shape[1] // 2, axis=1)


def kernel(
    nz, nf, slots, rb, edge, sr,
    rows, cols, count, values, rs, ridge, sol_out, res_out,
    vt, run_a, run_b, panel_a, panel_b, chosen_a, chosen_b, product_a, product_b, slabs, part, sib, pair, zbuf, dirs, img, rbuf,
    r_f32, g_f32, i_f32, link, sc_src, sc_feat, sc_mid, sc_comp, send_sems, recv_sems,
):
    comp, feat = lax.axis_index("comp"), lax.axis_index("feat")
    core, z = lax.rem(comp, 2), comp // 2
    low = edge // 2
    half = CB_DEV // 2 * low
    hp = nz * sr
    own_blocks = rb // nf
    sibling = {"comp": comp + 1 - 2 * core}
    n_comp = 2 * nz
    pending = []
    used = [0]
    mine = pl.ds(feat * own_blocks, own_blocks)

    def zpeer(k):
        return {"comp": lax.rem(z + k, nz) * 2 + core}

    def fpeer(k):
        return {"feat": lax.rem(feat + k, nf)}

    def cpeer(k):
        return {"comp": lax.rem(comp + k, n_comp)}

    def send(src, dst, device):
        at = used[0]
        used[0] += 1
        copy = pltpu.make_async_remote_copy(
            src_ref=src,
            dst_ref=dst,
            send_sem=send_sems.at[at],
            recv_sem=recv_sems.at[at],
            device_id=device,
            device_id_type=MESH,
        )
        copy.start()
        pending.append(copy)
        return copy

    def shard(k):
        return pl.multiple_of(lax.rem(z + k, nz) * sr, 16)

    prev_c, last_c = 0, slots
    prev_r, last_r = slots + CB_DEV, 2 * slots + CB_DEV

    def make_links(keys, groups, prev, last):
        seen = [jnp.int32(slots) for _ in range(groups)]
        live = count[0]
        for s in range(slots):
            key = keys[s]
            before = jnp.int32(slots)
            for q in range(groups):
                before = jnp.where(key == q, seen[q], before)
            link[prev + s] = before
            key = jnp.where(s < live, key, -1)
            for q in range(groups):
                seen[q] = jnp.where(key == q, s, seen[q])
        for q in range(groups):
            link[last + q] = seen[q]

    left = lax.broadcasted_iota(jnp.int32, (low, edge), 1) < low

    def swap(x):
        return pltpu.roll(x, low, axis=1)

    def widen(packed):
        x = packed.astype(F32)
        y = swap(x)
        zero = jnp.zeros_like(x)
        return jnp.concatenate(
            [
                jnp.where(left, x, zero).astype(BF16),
                jnp.where(left, y, zero).astype(BF16),
                jnp.where(left, zero, y).astype(BF16),
                jnp.where(left, zero, x).astype(BF16),
            ],
            axis=0,
        )

    def unpack(x0, x1):
        return jnp.where(left, x0, swap(x1)), jnp.where(left, swap(x0), x1)

    def column_sum(x):
        return jnp.sum(x, axis=0, keepdims=True)

    def stream(h):
        run = (run_a, run_b)[h]
        panel = (panel_a, panel_b)[h]
        chosen = (chosen_a, chosen_b)[h]
        product = (product_a, product_b)[h]

        def gather_feat(it):
            at = (it, h, mine)
            return [send(slabs.at[at], slabs.at[at], fpeer(k)) for k in range(1, nf)]

        def products(blocks, places, prev):
            for s in range(slots):
                chosen[s] = panel[places[s]]
            for s in range(slots):
                block = jnp.concatenate([blocks[s, :low], blocks[s, low:]], axis=1)
                product[s] = jnp.dot(block, widen(chosen[s]), preferred_element_type=F32)
            for s in range(slots):
                run[s] = product[s] + run[link[prev + s]]

        def backward(it):
            for r in range(rb):
                panel[r] = slabs[it, h, r]
            products(vt, rows, prev_c)
            for q in range(CB_DEV):
                d, p = q // (CB_DEV // 2), q % (CB_DEV // 2)
                part[it, h, pl.ds(d * hp + p * low, low)] = run[link[last_c + q]]
            if hp > half:
                for d in range(2):
                    part[it, h, pl.ds(d * hp + half, hp - half)] = jnp.zeros((hp - half, edge), F32)

        def scatter_comp(it):
            order = list(range(1, nz)) + [0]
            halves = {}
            for k in order:
                theirs = pl.multiple_of((1 - core) * hp + shard(k), 16)
                halves[k] = send(
                    part.at[it, h, pl.ds(theirs, sr)], sib.at[it, h, pl.ds(shard(k), sr)], sibling
                )
            yield
            arrivals = []
            total = None
            for k in order:
                halves[k].wait_recv()
                ours = pl.multiple_of(core * hp + shard(k), 16)
                both = part[it, h, pl.ds(ours, sr)] + sib[it, h, pl.ds(shard(k), sr)]
                if k:
                    pair[it, h, k] = both.astype(BF16)
                    arrivals.append(send(pair.at[it, h, k], zbuf.at[it, h, k], zpeer(k)))
                else:
                    total = both
            yield
            for k, copy in zip(order, arrivals):
                copy.wait_recv()
                total = total + zbuf[it, h, k].astype(F32)
            return total

        def gather_comp(it, piece):
            here = (it, h, pl.ds(pl.multiple_of(core * hp + shard(0), 16), sr))
            dirs[here] = piece.astype(BF16)
            across = [send(dirs.at[here], dirs.at[here], zpeer(k)) for k in range(1, nz)]
            beside = [send(dirs.at[here], dirs.at[here], sibling)]
            yield
            for k, copy in zip(range(1, nz), across):
                copy.wait_recv()
                came = (it, h, pl.ds(pl.multiple_of(core * hp + shard(nz - k), 16), sr))
                beside.append(send(dirs.at[came], dirs.at[came], sibling))
            yield
            for copy in beside:
                copy.wait_recv()

        def forward(it):
            for q in range(CB_DEV):
                d, p = q // (CB_DEV // 2), q % (CB_DEV // 2)
                panel[q] = dirs[it, h, pl.ds(d * hp + p * low, low)]
            products(values, cols, prev_r)
            for r in range(rb):
                img[it, h, r] = run[link[last_r + r]].astype(BF16)

        def scatter_feat(it):
            copies = [
                send(
                    img.at[it, h, pl.ds(lax.rem(feat + k, nf) * own_blocks, own_blocks)],
                    rbuf.at[it, h, k],
                    fpeer(k),
                )
                for k in range(1, nf)
            ]
            yield
            total = img[it, h, mine].astype(F32)
            for k, copy in zip(range(1, nf), copies):
                copy.wait_recv()
                total = total + rbuf[it, h, k].astype(F32)
            return total.reshape(own_blocks * low, edge)

        def sums(it, parts):
            for i, row in enumerate(parts):
                sc_src[it, h, pl.ds(i, 1)] = row
            copies = [
                send(sc_src.at[it, h], sc_feat.at[it, h, k], fpeer(k)) for k in range(1, nf)
            ]
            yield
            total = sc_src[it, h]
            for k, copy in zip(range(1, nf), copies):
                copy.wait_recv()
                total = total + sc_feat[it, h, k]
            sc_mid[it, h] = total
            copies = [
                send(sc_mid.at[it, h], sc_comp.at[it, h, k], cpeer(k)) for k in range(1, n_comp)
            ]
            yield
            for k, copy in zip(range(1, n_comp), copies):
                copy.wait_recv()
                total = total + sc_comp[it, h, k]
            return fold(total)

        copies = gather_feat(0)
        yield
        for copy in copies:
            copy.wait_recv()
        backward(0)
        g0 = yield from scatter_comp(0)
        g_f32[h] = g0
        yield from gather_comp(0, g0)
        forward(0)
        i0 = yield from scatter_feat(0)
        i_f32[h] = i0
        g0 = g_f32[h]
        first = yield from sums(0, [column_sum(i0 * i0), column_sum(g0 * g0)])
        penalty = ridge[pl.ds(h, 1)]
        image0, energy0 = first[0:1], first[1:2]
        step0 = energy0 / (image0 + penalty * energy0)
        r1 = r_f32[h] - step0 * i_f32[h]
        slabs[1, h, mine] = r1.astype(BF16).reshape(own_blocks, low, edge)
        copies = gather_feat(1)
        yield
        for copy in copies:
            copy.wait_recv()
        backward(1)
        g1 = yield from scatter_comp(1)
        g0 = g_f32[h]
        g1 = g1 - penalty * (step0 * g0)
        energy_row, mixed_row = column_sum(g1 * g1), column_sum(g1 * g0)
        yield from gather_comp(1, g1)
        forward(1)
        u = yield from scatter_feat(1)
        i0 = i_f32[h]
        last = yield from sums(
            1, [column_sum(u * u), column_sum(u * i0), energy_row, mixed_row]
        )
        uu, ui, energy1, gg = last[0:1], last[1:2], last[2:3], last[3:4]
        beta = energy1 / energy0
        curvature = (
            uu + beta * (2.0 * ui + beta * image0)
            + penalty * (energy1 + beta * (2.0 * gg + beta * energy0))
        )
        step1 = energy1 / curvature
        weight = step0 + step1 * beta
        r_f32[h] = r_f32[h] - weight * i_f32[h] - step1 * u
        return weight, step1

    barrier = pltpu.get_barrier_semaphore()
    for k in range(1, n_comp):
        pl.semaphore_signal(barrier, inc=1, device_id=cpeer(k), device_id_type=MESH)
    for k in range(1, nf):
        pl.semaphore_signal(barrier, inc=1, device_id=fpeer(k), device_id_type=MESH)
    for r in range(own_blocks):
        top, bottom = rs[pl.ds(r * edge, low)], rs[pl.ds(r * edge + low, low)]
        for h, x in enumerate(unpack(top, bottom)):
            r_f32[h, pl.ds(r * low, low)] = x
    for h in range(2):
        slabs[0, h, mine] = r_f32[h].astype(BF16).reshape(own_blocks, low, edge)
    sc_src[...] = jnp.zeros_like(sc_src)
    pl.semaphore_wait(barrier, n_comp - 1 + nf - 1)

    streams = [stream(h) for h in range(2)]
    steps = [None, None]
    for g in streams:
        next(g)
    run_a[slots] = jnp.zeros((low, edge), F32)
    run_b[slots] = jnp.zeros((low, edge), F32)
    for s in range(slots):
        vt[s] = values[s].T
    make_links(cols, CB_DEV, prev_c, last_c)
    make_links(rows, rb, prev_r, last_r)
    while None in steps:
        for h, g in enumerate(streams):
            try:
                next(g)
            except StopIteration as done:
                steps[h] = done.value
    for r in range(own_blocks):
        parts = unpack(r_f32[0, pl.ds(r * low, low)], r_f32[1, pl.ds(r * low, low)])
        for d in range(2):
            res_out[pl.ds(r * edge + d * low, low)] = parts[d]
    for q in range(CB_DEV):
        d, p = q // (CB_DEV // 2), q % (CB_DEV // 2)
        take = pl.ds(d * hp + p * low, low)
        found = [
            steps[h][0] * dirs[0, h, take].astype(F32) + steps[h][1] * dirs[1, h, take].astype(F32)
            for h in range(2)
        ]
        parts = unpack(*found)
        for d in range(2):
            sol_out[pl.ds(q * edge + d * low, low)] = parts[d]
    for copy in pending:
        copy.wait_send()


def shards(nz, nf, block_values, block_rows, block_cols, block_counts, right_side, ridge):
    values = block_values[0, 0]
    rows, cols, count = block_rows[0, 0], block_cols[0, 0], block_counts[0]
    slots, edge = values.shape[0], values.shape[1]
    held = right_side.shape[0]
    rb = held * nf // edge
    low = edge // 2
    sr = -(-(CB_DEV // 2 * low) // (nz * 16)) * 16
    hp = nz * sr
    own = rb // nf
    n_copies = 4 * (2 * (nf - 1) + 2 * (nz - 1) + 2 * nz + (nf - 1) + (2 * nz - 1))
    penalties = jnp.tile(ridge.reshape(2, low), (1, 2))
    smem = pl.BlockSpec(memory_space=pltpu.SMEM)
    vmem = pl.BlockSpec(memory_space=pltpu.VMEM)
    return pl.pallas_call(
        functools.partial(kernel, nz, nf, slots, rb, edge, sr),
        out_shape=(
            jax.ShapeDtypeStruct((CB_DEV * edge, edge), F32),
            jax.ShapeDtypeStruct((held, edge), F32),
        ),
        in_specs=[smem, smem, smem, vmem, vmem, vmem],
        out_specs=(vmem, vmem),
        scratch_shapes=[
            pltpu.VMEM((slots, edge, edge), BF16),
            pltpu.VMEM((slots + 1, low, edge), F32),
            pltpu.VMEM((slots + 1, low, edge), F32),
            pltpu.VMEM((max(rb, CB_DEV), low, edge), BF16),
            pltpu.VMEM((max(rb, CB_DEV), low, edge), BF16),
            pltpu.VMEM((slots, low, edge), BF16),
            pltpu.VMEM((slots, low, edge), BF16),
            pltpu.VMEM((slots, low, edge), F32),
            pltpu.VMEM((slots, low, edge), F32),
            pltpu.VMEM((2, 2, rb, low, edge), BF16),
            pltpu.VMEM((2, 2, 2 * hp, edge), F32),
            pltpu.VMEM((2, 2, hp, edge), F32),
            pltpu.VMEM((2, 2, nz, sr, edge), BF16),
            pltpu.VMEM((2, 2, nz, sr, edge), BF16),
            pltpu.VMEM((2, 2, 2 * hp, edge), BF16),
            pltpu.VMEM((2, 2, rb, low, edge), BF16),
            pltpu.VMEM((2, 2, nf, own, low, edge), BF16),
            pltpu.VMEM((2, own * low, edge), F32),
            pltpu.VMEM((2, sr, edge), F32),
            pltpu.VMEM((2, own * low, edge), F32),
            pltpu.SMEM((2 * slots + CB_DEV + rb,), jnp.int32),
            pltpu.VMEM((2, 2, 8, edge), F32),
            pltpu.VMEM((2, 2, nf, 8, edge), F32),
            pltpu.VMEM((2, 2, 8, edge), F32),
            pltpu.VMEM((2, 2, 2 * nz, 8, edge), F32),
            pltpu.SemaphoreType.DMA((n_copies,)),
            pltpu.SemaphoreType.DMA((n_copies,)),
        ],
        compiler_params=pltpu.CompilerParams(
            collective_id=0, has_side_effects=True, vmem_limit_bytes=48 * 1024 * 1024
        ),
        cost_estimate=pl.CostEstimate(
            flops=8 * slots * edge**3, bytes_accessed=4 * 1024 * 1024, transcendentals=0
        ),
    )(rows, cols, count, values, right_side, penalties)


def solution(mesh):
    nz, nf = mesh.shape["comp"] // 2, mesh.shape["feat"]
    placed = (
        P("comp", "feat", None, None, None),
        P("comp", "feat", None),
        P("comp", "feat", None),
        P("comp", "feat"),
        P(("comp", "feat"), None),
        P(),
    )
    return jax.shard_map(
        functools.partial(shards, nz, nf),
        mesh=mesh,
        in_specs=placed,
        out_specs=(P("feat", None), P(("comp", "feat"), None)),
        check_vma=False,
    )
```

```python
import functools

import jax
import jax.numpy as jnp
from jax import lax
from jax.experimental import pallas as pl
from jax.experimental.pallas import tpu as pltpu
from jax.sharding import PartitionSpec as P

CB_DEV = 14
MESH = pl.DeviceIdType.MESH
F32 = jnp.float32
BF16 = jnp.bfloat16


def fold(x):
    return x + pltpu.roll(x, x.shape[1] // 2, axis=1)


def kernel(
    nz, nf, slots, rb, edge, sr,
    rows, cols, count, values, rs, ridge, sol_out, res_out,
    vt, run_a, run_b, panel_a, panel_b, chosen_a, chosen_b, product_a, product_b, slabs, part, sib, pair, zbuf, dirs, img, rbuf,
    r_f32, g_f32, i_f32, link, sc_src, sc_feat, sc_mid, sc_comp, send_sems, recv_sems,
):
    comp, feat = lax.axis_index("comp"), lax.axis_index("feat")
    core, z = lax.rem(comp, 2), comp // 2
    low = edge // 2
    half = CB_DEV // 2 * low
    hp = nz * sr
    own_blocks = rb // nf
    sibling = {"comp": comp + 1 - 2 * core}
    n_comp = 2 * nz
    pending = []
    used = [0]
    mine = pl.ds(feat * own_blocks, own_blocks)

    def zpeer(k):
        return {"comp": lax.rem(z + k, nz) * 2 + core}

    def fpeer(k):
        return {"feat": lax.rem(feat + k, nf)}

    def cpeer(k):
        return {"comp": lax.rem(comp + k, n_comp)}

    def send(src, dst, device):
        at = used[0]
        used[0] += 1
        copy = pltpu.make_async_remote_copy(
            src_ref=src,
            dst_ref=dst,
            send_sem=send_sems.at[at],
            recv_sem=recv_sems.at[at],
            device_id=device,
            device_id_type=MESH,
        )
        copy.start()
        pending.append(copy)
        return copy

    def shard(k):
        return pl.multiple_of(lax.rem(z + k, nz) * sr, 16)

    prev_c, last_c = 0, slots
    prev_r, last_r = slots + CB_DEV, 2 * slots + CB_DEV

    def make_links(keys, groups, prev, last):
        seen = [jnp.int32(slots) for _ in range(groups)]
        live = count[0]
        for s in range(slots):
            key = keys[s]
            before = jnp.int32(slots)
            for q in range(groups):
                before = jnp.where(key == q, seen[q], before)
            link[prev + s] = before
            key = jnp.where(s < live, key, -1)
            for q in range(groups):
                seen[q] = jnp.where(key == q, s, seen[q])
        for q in range(groups):
            link[last + q] = seen[q]

    left = lax.broadcasted_iota(jnp.int32, (low, edge), 1) < low

    def swap(x):
        return pltpu.roll(x, low, axis=1)

    def widen(packed):
        x = packed.astype(F32)
        y = swap(x)
        zero = jnp.zeros_like(x)
        return jnp.concatenate(
            [
                jnp.where(left, x, zero).astype(BF16),
                jnp.where(left, y, zero).astype(BF16),
                jnp.where(left, zero, y).astype(BF16),
                jnp.where(left, zero, x).astype(BF16),
            ],
            axis=0,
        )

    def unpack(x0, x1):
        return jnp.where(left, x0, swap(x1)), jnp.where(left, swap(x0), x1)

    def column_sum(x):
        return jnp.sum(x, axis=0, keepdims=True)

    def stream(h):
        run = (run_a, run_b)[h]
        panel = (panel_a, panel_b)[h]
        chosen = (chosen_a, chosen_b)[h]
        product = (product_a, product_b)[h]

        def gather_feat(it):
            at = (it, h, mine)
            return [send(slabs.at[at], slabs.at[at], fpeer(k)) for k in range(1, nf)]

        def products(blocks, places, prev):
            for s in range(slots):
                chosen[s] = panel[places[s]]
            for s in range(slots):
                block = jnp.concatenate([blocks[s, :low], blocks[s, low:]], axis=1)
                product[s] = jnp.dot(block, widen(chosen[s]), preferred_element_type=F32)
            for s in range(slots):
                run[s] = product[s] + run[link[prev + s]]

        def backward(it):
            for r in range(rb):
                panel[r] = slabs[it, h, r]
            products(vt, rows, prev_c)
            for q in range(CB_DEV):
                d, p = q // (CB_DEV // 2), q % (CB_DEV // 2)
                part[it, h, pl.ds(d * hp + p * low, low)] = run[link[last_c + q]]
            if hp > half:
                for d in range(2):
                    part[it, h, pl.ds(d * hp + half, hp - half)] = jnp.zeros((hp - half, edge), F32)

        def scatter_comp(it):
            order = list(range(1, nz)) + [0]
            halves = {}
            for k in order:
                theirs = pl.multiple_of((1 - core) * hp + shard(k), 16)
                halves[k] = send(
                    part.at[it, h, pl.ds(theirs, sr)], sib.at[it, h, pl.ds(shard(k), sr)], sibling
                )
            yield
            arrivals = []
            total = None
            for k in order:
                halves[k].wait_recv()
                ours = pl.multiple_of(core * hp + shard(k), 16)
                both = part[it, h, pl.ds(ours, sr)] + sib[it, h, pl.ds(shard(k), sr)]
                if k:
                    pair[it, h, k] = both.astype(BF16)
                    arrivals.append(send(pair.at[it, h, k], zbuf.at[it, h, k], zpeer(k)))
                else:
                    total = both
            yield
            for k, copy in zip(order, arrivals):
                copy.wait_recv()
                total = total + zbuf[it, h, k].astype(F32)
            return total

        def gather_comp(it, piece):
            here = (it, h, pl.ds(pl.multiple_of(core * hp + shard(0), 16), sr))
            dirs[here] = piece.astype(BF16)
            across = [send(dirs.at[here], dirs.at[here], zpeer(k)) for k in range(1, nz)]
            beside = [send(dirs.at[here], dirs.at[here], sibling)]
            yield
            for k, copy in zip(range(1, nz), across):
                copy.wait_recv()
                came = (it, h, pl.ds(pl.multiple_of(core * hp + shard(nz - k), 16), sr))
                beside.append(send(dirs.at[came], dirs.at[came], sibling))
            yield
            for copy in beside:
                copy.wait_recv()

        def forward(it):
            for q in range(CB_DEV):
                d, p = q // (CB_DEV // 2), q % (CB_DEV // 2)
                panel[q] = dirs[it, h, pl.ds(d * hp + p * low, low)]
            products(values, cols, prev_r)
            for r in range(rb):
                img[it, h, r] = run[link[last_r + r]].astype(BF16)

        def scatter_feat(it):
            copies = [
                send(
                    img.at[it, h, pl.ds(lax.rem(feat + k, nf) * own_blocks, own_blocks)],
                    rbuf.at[it, h, k],
                    fpeer(k),
                )
                for k in range(1, nf)
            ]
            yield
            total = img[it, h, mine].astype(F32)
            for k, copy in zip(range(1, nf), copies):
                copy.wait_recv()
                total = total + rbuf[it, h, k].astype(F32)
            return total.reshape(own_blocks * low, edge)

        def sums(it, parts):
            for i, row in enumerate(parts):
                sc_src[it, h, pl.ds(i, 1)] = row
            copies = [
                send(sc_src.at[it, h], sc_feat.at[it, h, k], fpeer(k)) for k in range(1, nf)
            ]
            yield
            total = sc_src[it, h]
            for k, copy in zip(range(1, nf), copies):
                copy.wait_recv()
                total = total + sc_feat[it, h, k]
            sc_mid[it, h] = total
            copies = [
                send(sc_mid.at[it, h], sc_comp.at[it, h, k], cpeer(k)) for k in range(1, n_comp)
            ]
            yield
            for k, copy in zip(range(1, n_comp), copies):
                copy.wait_recv()
                total = total + sc_comp[it, h, k]
            return fold(total)

        copies = gather_feat(0)
        yield
        for copy in copies:
            copy.wait_recv()
        backward(0)
        g0 = yield from scatter_comp(0)
        g_f32[h] = g0
        yield from gather_comp(0, g0)
        forward(0)
        i0 = yield from scatter_feat(0)
        i_f32[h] = i0
        g0 = g_f32[h]
        first = yield from sums(0, [column_sum(i0 * i0), column_sum(g0 * g0)])
        penalty = ridge[pl.ds(h, 1)]
        image0, energy0 = first[0:1], first[1:2]
        step0 = energy0 / (image0 + penalty * energy0)
        r1 = r_f32[h] - step0 * i_f32[h]
        slabs[1, h, mine] = r1.astype(BF16).reshape(own_blocks, low, edge)
        copies = gather_feat(1)
        yield
        for copy in copies:
            copy.wait_recv()
        backward(1)
        g1 = yield from scatter_comp(1)
        g0 = g_f32[h]
        g1 = g1 - penalty * (step0 * g0)
        energy_row, mixed_row = column_sum(g1 * g1), column_sum(g1 * g0)
        yield from gather_comp(1, g1)
        forward(1)
        u = yield from scatter_feat(1)
        i0 = i_f32[h]
        last = yield from sums(
            1, [column_sum(u * u), column_sum(u * i0), energy_row, mixed_row]
        )
        uu, ui, energy1, gg = last[0:1], last[1:2], last[2:3], last[3:4]
        beta = energy1 / energy0
        curvature = (
            uu + beta * (2.0 * ui + beta * image0)
            + penalty * (energy1 + beta * (2.0 * gg + beta * energy0))
        )
        step1 = energy1 / curvature
        weight = step0 + step1 * beta
        r_f32[h] = r_f32[h] - weight * i_f32[h] - step1 * u
        return weight, step1

    barrier = pltpu.get_barrier_semaphore()
    for k in range(1, n_comp):
        pl.semaphore_signal(barrier, inc=1, device_id=cpeer(k), device_id_type=MESH)
    for k in range(1, nf):
        pl.semaphore_signal(barrier, inc=1, device_id=fpeer(k), device_id_type=MESH)
    for r in range(own_blocks):
        top, bottom = rs[pl.ds(r * edge, low)], rs[pl.ds(r * edge + low, low)]
        for h, x in enumerate(unpack(top, bottom)):
            r_f32[h, pl.ds(r * low, low)] = x
    for h in range(2):
        slabs[0, h, mine] = r_f32[h].astype(BF16).reshape(own_blocks, low, edge)
    sc_src[...] = jnp.zeros_like(sc_src)
    pl.semaphore_wait(barrier, n_comp - 1 + nf - 1)

    streams = [stream(h) for h in range(2)]
    steps = [None, None]
    next(streams[0])
    run_a[slots] = jnp.zeros((low, edge), F32)
    run_b[slots] = jnp.zeros((low, edge), F32)
    for s in range(slots):
        vt[s] = values[s].T
    make_links(cols, CB_DEV, prev_c, last_c)
    make_links(rows, rb, prev_r, last_r)
    next(streams[0])
    while None in steps:
        for h, g in reversed(list(enumerate(streams))):
            if steps[h] is not None:
                continue
            try:
                next(g)
            except StopIteration as done:
                steps[h] = done.value
    for r in range(own_blocks):
        parts = unpack(r_f32[0, pl.ds(r * low, low)], r_f32[1, pl.ds(r * low, low)])
        for d in range(2):
            res_out[pl.ds(r * edge + d * low, low)] = parts[d]
    for q in range(CB_DEV):
        d, p = q // (CB_DEV // 2), q % (CB_DEV // 2)
        take = pl.ds(d * hp + p * low, low)
        found = [
            steps[h][0] * dirs[0, h, take].astype(F32) + steps[h][1] * dirs[1, h, take].astype(F32)
            for h in range(2)
        ]
        parts = unpack(*found)
        for d in range(2):
            sol_out[pl.ds(q * edge + d * low, low)] = parts[d]
    for copy in pending:
        copy.wait_send()


def shards(nz, nf, block_values, block_rows, block_cols, block_counts, right_side, ridge):
    values = block_values[0, 0]
    rows, cols, count = block_rows[0, 0], block_cols[0, 0], block_counts[0]
    slots, edge = values.shape[0], values.shape[1]
    held = right_side.shape[0]
    rb = held * nf // edge
    low = edge // 2
    sr = -(-(CB_DEV // 2 * low) // (nz * 16)) * 16
    hp = nz * sr
    own = rb // nf
    n_copies = 4 * (2 * (nf - 1) + 2 * (nz - 1) + 2 * nz + (nf - 1) + (2 * nz - 1))
    penalties = jnp.tile(ridge.reshape(2, low), (1, 2))
    smem = pl.BlockSpec(memory_space=pltpu.SMEM)
    vmem = pl.BlockSpec(memory_space=pltpu.VMEM)
    return pl.pallas_call(
        functools.partial(kernel, nz, nf, slots, rb, edge, sr),
        out_shape=(
            jax.ShapeDtypeStruct((CB_DEV * edge, edge), F32),
            jax.ShapeDtypeStruct((held, edge), F32),
        ),
        in_specs=[smem, smem, smem, vmem, vmem, vmem],
        out_specs=(vmem, vmem),
        scratch_shapes=[
            pltpu.VMEM((slots, edge, edge), BF16),
            pltpu.VMEM((slots + 1, low, edge), F32),
            pltpu.VMEM((slots + 1, low, edge), F32),
            pltpu.VMEM((max(rb, CB_DEV), low, edge), BF16),
            pltpu.VMEM((max(rb, CB_DEV), low, edge), BF16),
            pltpu.VMEM((slots, low, edge), BF16),
            pltpu.VMEM((slots, low, edge), BF16),
            pltpu.VMEM((slots, low, edge), F32),
            pltpu.VMEM((slots, low, edge), F32),
            pltpu.VMEM((2, 2, rb, low, edge), BF16),
            pltpu.VMEM((2, 2, 2 * hp, edge), F32),
            pltpu.VMEM((2, 2, hp, edge), F32),
            pltpu.VMEM((2, 2, nz, sr, edge), BF16),
            pltpu.VMEM((2, 2, nz, sr, edge), BF16),
            pltpu.VMEM((2, 2, 2 * hp, edge), BF16),
            pltpu.VMEM((2, 2, rb, low, edge), BF16),
            pltpu.VMEM((2, 2, nf, own, low, edge), BF16),
            pltpu.VMEM((2, own * low, edge), F32),
            pltpu.VMEM((2, sr, edge), F32),
            pltpu.VMEM((2, own * low, edge), F32),
            pltpu.SMEM((2 * slots + CB_DEV + rb,), jnp.int32),
            pltpu.VMEM((2, 2, 8, edge), F32),
            pltpu.VMEM((2, 2, nf, 8, edge), F32),
            pltpu.VMEM((2, 2, 8, edge), F32),
            pltpu.VMEM((2, 2, 2 * nz, 8, edge), F32),
            pltpu.SemaphoreType.DMA((n_copies,)),
            pltpu.SemaphoreType.DMA((n_copies,)),
        ],
        compiler_params=pltpu.CompilerParams(
            collective_id=0, has_side_effects=True, vmem_limit_bytes=48 * 1024 * 1024
        ),
        cost_estimate=pl.CostEstimate(
            flops=8 * slots * edge**3, bytes_accessed=4 * 1024 * 1024, transcendentals=0
        ),
    )(rows, cols, count, values, right_side, penalties)


def solution(mesh):
    nz, nf = mesh.shape["comp"] // 2, mesh.shape["feat"]
    placed = (
        P("comp", "feat", None, None, None),
        P("comp", "feat", None),
        P("comp", "feat", None),
        P("comp", "feat"),
        P(("comp", "feat"), None),
        P(),
    )
    return jax.shard_map(
        functools.partial(shards, nz, nf),
        mesh=mesh,
        in_specs=placed,
        out_specs=(P("feat", None), P(("comp", "feat"), None)),
        check_vma=False,
    )
```

```python
import functools

import jax
import jax.numpy as jnp
from jax import lax
from jax.experimental import pallas as pl
from jax.experimental.pallas import tpu as pltpu
from jax.sharding import PartitionSpec as P

CB_DEV = 14
MESH = pl.DeviceIdType.MESH
F32 = jnp.float32
BF16 = jnp.bfloat16


def fold(x):
    return x + pltpu.roll(x, x.shape[1] // 2, axis=1)


def kernel(
    nz, nf, slots, rb, edge, sr,
    rows, cols, count, values_in, rs_in, ridge, sol_out, res_out,
    values, rs, vt, run_a, run_b, panel_a, panel_b, chosen_a, chosen_b, product_a, product_b, slabs, part, sib, pair, zbuf, dirs, img, rbuf,
    r_f32, g_f32, i_f32, link, sc_src, sc_feat, sc_mid, sc_comp, load_sems, send_sems, recv_sems,
):
    comp, feat = lax.axis_index("comp"), lax.axis_index("feat")
    core, z = lax.rem(comp, 2), comp // 2
    low = edge // 2
    half = CB_DEV // 2 * low
    hp = nz * sr
    own_blocks = rb // nf
    sibling = {"comp": comp + 1 - 2 * core}
    n_comp = 2 * nz
    pending = []
    used = [0]
    mine = pl.ds(feat * own_blocks, own_blocks)

    def zpeer(k):
        return {"comp": lax.rem(z + k, nz) * 2 + core}

    def fpeer(k):
        return {"feat": lax.rem(feat + k, nf)}

    def cpeer(k):
        return {"comp": lax.rem(comp + k, n_comp)}

    def send(src, dst, device):
        at = used[0]
        used[0] += 1
        copy = pltpu.make_async_remote_copy(
            src_ref=src,
            dst_ref=dst,
            send_sem=send_sems.at[at],
            recv_sem=recv_sems.at[at],
            device_id=device,
            device_id_type=MESH,
        )
        copy.start()
        pending.append(copy)
        return copy

    def shard(k):
        return pl.multiple_of(lax.rem(z + k, nz) * sr, 16)

    prev_c, last_c = 0, slots
    prev_r, last_r = slots + CB_DEV, 2 * slots + CB_DEV

    def make_links(keys, groups, prev, last):
        seen = [jnp.int32(slots) for _ in range(groups)]
        live = count[0]
        for s in range(slots):
            key = keys[s]
            before = jnp.int32(slots)
            for q in range(groups):
                before = jnp.where(key == q, seen[q], before)
            link[prev + s] = before
            key = jnp.where(s < live, key, -1)
            for q in range(groups):
                seen[q] = jnp.where(key == q, s, seen[q])
        for q in range(groups):
            link[last + q] = seen[q]

    left = lax.broadcasted_iota(jnp.int32, (low, edge), 1) < low

    def swap(x):
        return pltpu.roll(x, low, axis=1)

    def widen(packed):
        x = packed.astype(F32)
        y = swap(x)
        zero = jnp.zeros_like(x)
        return jnp.concatenate(
            [
                jnp.where(left, x, zero).astype(BF16),
                jnp.where(left, y, zero).astype(BF16),
                jnp.where(left, zero, y).astype(BF16),
                jnp.where(left, zero, x).astype(BF16),
            ],
            axis=0,
        )

    def unpack(x0, x1):
        return jnp.where(left, x0, swap(x1)), jnp.where(left, swap(x0), x1)

    def column_sum(x):
        return jnp.sum(x, axis=0, keepdims=True)

    def stream(h):
        run = (run_a, run_b)[h]
        panel = (panel_a, panel_b)[h]
        chosen = (chosen_a, chosen_b)[h]
        product = (product_a, product_b)[h]

        def gather_feat(it):
            at = (it, h, mine)
            return [send(slabs.at[at], slabs.at[at], fpeer(k)) for k in range(1, nf)]

        def products(blocks, places, prev):
            for s in range(slots):
                chosen[s] = panel[places[s]]
            for s in range(slots):
                block = jnp.concatenate([blocks[s, :low], blocks[s, low:]], axis=1)
                product[s] = jnp.dot(block, widen(chosen[s]), preferred_element_type=F32)
            for s in range(slots):
                run[s] = product[s] + run[link[prev + s]]

        def backward(it):
            for r in range(rb):
                panel[r] = slabs[it, h, r]
            products(vt, rows, prev_c)
            for q in range(CB_DEV):
                d, p = q // (CB_DEV // 2), q % (CB_DEV // 2)
                part[it, h, pl.ds(d * hp + p * low, low)] = run[link[last_c + q]]
            if hp > half:
                for d in range(2):
                    part[it, h, pl.ds(d * hp + half, hp - half)] = jnp.zeros((hp - half, edge), F32)

        def scatter_comp(it):
            order = list(range(1, nz)) + [0]
            theirs = pl.multiple_of((1 - core) * hp, 16)
            whole = send(part.at[it, h, pl.ds(theirs, hp)], sib.at[it, h], sibling)
            yield
            arrivals = []
            total = None
            whole.wait_recv()
            for k in order:
                ours = pl.multiple_of(core * hp + shard(k), 16)
                both = part[it, h, pl.ds(ours, sr)] + sib[it, h, pl.ds(shard(k), sr)]
                if k:
                    pair[it, h, k] = both.astype(BF16)
                    arrivals.append(send(pair.at[it, h, k], zbuf.at[it, h, k], zpeer(k)))
                else:
                    total = both
            yield
            for k, copy in zip(order, arrivals):
                copy.wait_recv()
                total = total + zbuf[it, h, k].astype(F32)
            return total

        def gather_comp(it, piece):
            here = (it, h, pl.ds(pl.multiple_of(core * hp + shard(0), 16), sr))
            dirs[here] = piece.astype(BF16)
            across = [send(dirs.at[here], dirs.at[here], zpeer(k)) for k in range(1, nz)]
            yield
            for copy in across:
                copy.wait_recv()
            ours = (it, h, pl.ds(pl.multiple_of(core * hp, 16), hp))
            beside = send(dirs.at[ours], dirs.at[ours], sibling)
            yield
            beside.wait_recv()

        def forward(it):
            for q in range(CB_DEV):
                d, p = q // (CB_DEV // 2), q % (CB_DEV // 2)
                panel[q] = dirs[it, h, pl.ds(d * hp + p * low, low)]
            products(values, cols, prev_r)
            for r in range(rb):
                img[it, h, r] = run[link[last_r + r]].astype(BF16)

        def scatter_feat(it):
            copies = [
                send(
                    img.at[it, h, pl.ds(lax.rem(feat + k, nf) * own_blocks, own_blocks)],
                    rbuf.at[it, h, k],
                    fpeer(k),
                )
                for k in range(1, nf)
            ]
            yield
            total = img[it, h, mine].astype(F32)
            for k, copy in zip(range(1, nf), copies):
                copy.wait_recv()
                total = total + rbuf[it, h, k].astype(F32)
            return total.reshape(own_blocks * low, edge)

        def sums(it, parts):
            for i, row in enumerate(parts):
                sc_src[it, h, pl.ds(i, 1)] = row
            copies = [
                send(sc_src.at[it, h], sc_feat.at[it, h, k], fpeer(k)) for k in range(1, nf)
            ]
            yield
            total = sc_src[it, h]
            for k, copy in zip(range(1, nf), copies):
                copy.wait_recv()
                total = total + sc_feat[it, h, k]
            sc_mid[it, h] = total
            copies = [
                send(sc_mid.at[it, h], sc_comp.at[it, h, k], cpeer(k)) for k in range(1, n_comp)
            ]
            yield
            for k, copy in zip(range(1, n_comp), copies):
                copy.wait_recv()
                total = total + sc_comp[it, h, k]
            return fold(total)

        copies = gather_feat(0)
        yield
        for copy in copies:
            copy.wait_recv()
        backward(0)
        g0 = yield from scatter_comp(0)
        g_f32[h] = g0
        yield from gather_comp(0, g0)
        forward(0)
        i0 = yield from scatter_feat(0)
        i_f32[h] = i0
        g0 = g_f32[h]
        first = yield from sums(0, [column_sum(i0 * i0), column_sum(g0 * g0)])
        penalty = ridge[pl.ds(h, 1)]
        image0, energy0 = first[0:1], first[1:2]
        step0 = energy0 / (image0 + penalty * energy0)
        r1 = r_f32[h] - step0 * i_f32[h]
        slabs[1, h, mine] = r1.astype(BF16).reshape(own_blocks, low, edge)
        copies = gather_feat(1)
        yield
        for copy in copies:
            copy.wait_recv()
        backward(1)
        g1 = yield from scatter_comp(1)
        g0 = g_f32[h]
        g1 = g1 - penalty * (step0 * g0)
        energy_row, mixed_row = column_sum(g1 * g1), column_sum(g1 * g0)
        yield from gather_comp(1, g1)
        forward(1)
        u = yield from scatter_feat(1)
        i0 = i_f32[h]
        last = yield from sums(
            1, [column_sum(u * u), column_sum(u * i0), energy_row, mixed_row]
        )
        uu, ui, energy1, gg = last[0:1], last[1:2], last[2:3], last[3:4]
        beta = energy1 / energy0
        curvature = (
            uu + beta * (2.0 * ui + beta * image0)
            + penalty * (energy1 + beta * (2.0 * gg + beta * energy0))
        )
        step1 = energy1 / curvature
        weight = step0 + step1 * beta
        r_f32[h] = r_f32[h] - weight * i_f32[h] - step1 * u
        return weight, step1

    load_rs = pltpu.make_async_copy(rs_in, rs, load_sems.at[0])
    load_rs.start()
    load_values = pltpu.make_async_copy(values_in, values, load_sems.at[1])
    load_values.start()
    barrier = pltpu.get_barrier_semaphore()
    for k in range(1, n_comp):
        pl.semaphore_signal(barrier, inc=1, device_id=cpeer(k), device_id_type=MESH)
    for k in range(1, nf):
        pl.semaphore_signal(barrier, inc=1, device_id=fpeer(k), device_id_type=MESH)
    sc_src[...] = jnp.zeros_like(sc_src)
    load_rs.wait()
    for r in range(own_blocks):
        top, bottom = rs[pl.ds(r * edge, low)], rs[pl.ds(r * edge + low, low)]
        for h, x in enumerate(unpack(top, bottom)):
            r_f32[h, pl.ds(r * low, low)] = x
    for h in range(2):
        slabs[0, h, mine] = r_f32[h].astype(BF16).reshape(own_blocks, low, edge)
    pl.semaphore_wait(barrier, n_comp - 1 + nf - 1)

    streams = [stream(h) for h in range(2)]
    steps = [None, None]
    next(streams[0])
    run_a[slots] = jnp.zeros((low, edge), F32)
    run_b[slots] = jnp.zeros((low, edge), F32)
    make_links(cols, CB_DEV, prev_c, last_c)
    make_links(rows, rb, prev_r, last_r)
    load_values.wait()
    for s in range(slots):
        vt[s] = values[s].T
    next(streams[0])
    turns, done_sends = [0], 0
    while None in steps:
        for h, g in reversed(list(enumerate(streams))):
            if steps[h] is not None:
                continue
            turns.append(len(pending))
            while done_sends < turns[max(len(turns) - 4, 0)]:
                pending[done_sends].wait_send()
                done_sends += 1
            try:
                next(g)
            except StopIteration as done:
                steps[h] = done.value
    for r in range(own_blocks):
        parts = unpack(r_f32[0, pl.ds(r * low, low)], r_f32[1, pl.ds(r * low, low)])
        for d in range(2):
            res_out[pl.ds(r * edge + d * low, low)] = parts[d]
    for q in range(CB_DEV):
        d, p = q // (CB_DEV // 2), q % (CB_DEV // 2)
        take = pl.ds(d * hp + p * low, low)
        found = [
            steps[h][0] * dirs[0, h, take].astype(F32) + steps[h][1] * dirs[1, h, take].astype(F32)
            for h in range(2)
        ]
        parts = unpack(*found)
        for d in range(2):
            sol_out[pl.ds(q * edge + d * low, low)] = parts[d]
    for copy in pending[done_sends:]:
        copy.wait_send()


def shards(nz, nf, block_values, block_rows, block_cols, block_counts, right_side, ridge):
    values = block_values[0, 0]
    rows, cols, count = block_rows[0, 0], block_cols[0, 0], block_counts[0]
    slots, edge = values.shape[0], values.shape[1]
    held = right_side.shape[0]
    rb = held * nf // edge
    low = edge // 2
    sr = -(-(CB_DEV // 2 * low) // (nz * 16)) * 16
    hp = nz * sr
    own = rb // nf
    n_copies = 4 * (2 * (nf - 1) + 2 * (nz - 1) + 2 + (nf - 1) + (2 * nz - 1))
    penalties = jnp.tile(ridge.reshape(2, low), (1, 2))
    smem = pl.BlockSpec(memory_space=pltpu.SMEM)
    anywhere = pl.BlockSpec(memory_space=pl.ANY)
    vmem = pl.BlockSpec(memory_space=pltpu.VMEM)
    return pl.pallas_call(
        functools.partial(kernel, nz, nf, slots, rb, edge, sr),
        out_shape=(
            jax.ShapeDtypeStruct((CB_DEV * edge, edge), F32),
            jax.ShapeDtypeStruct((held, edge), F32),
        ),
        in_specs=[smem, smem, smem, anywhere, anywhere, vmem],
        out_specs=(vmem, vmem),
        scratch_shapes=[
            pltpu.VMEM((slots, edge, edge), BF16),
            pltpu.VMEM((held, edge), F32),
            pltpu.VMEM((slots, edge, edge), BF16),
            pltpu.VMEM((slots + 1, low, edge), F32),
            pltpu.VMEM((slots + 1, low, edge), F32),
            pltpu.VMEM((max(rb, CB_DEV), low, edge), BF16),
            pltpu.VMEM((max(rb, CB_DEV), low, edge), BF16),
            pltpu.VMEM((slots, low, edge), BF16),
            pltpu.VMEM((slots, low, edge), BF16),
            pltpu.VMEM((slots, low, edge), F32),
            pltpu.VMEM((slots, low, edge), F32),
            pltpu.VMEM((2, 2, rb, low, edge), BF16),
            pltpu.VMEM((2, 2, 2 * hp, edge), F32),
            pltpu.VMEM((2, 2, hp, edge), F32),
            pltpu.VMEM((2, 2, nz, sr, edge), BF16),
            pltpu.VMEM((2, 2, nz, sr, edge), BF16),
            pltpu.VMEM((2, 2, 2 * hp, edge), BF16),
            pltpu.VMEM((2, 2, rb, low, edge), BF16),
            pltpu.VMEM((2, 2, nf, own, low, edge), BF16),
            pltpu.VMEM((2, own * low, edge), F32),
            pltpu.VMEM((2, sr, edge), F32),
            pltpu.VMEM((2, own * low, edge), F32),
            pltpu.SMEM((2 * slots + CB_DEV + rb,), jnp.int32),
            pltpu.VMEM((2, 2, 8, edge), F32),
            pltpu.VMEM((2, 2, nf, 8, edge), F32),
            pltpu.VMEM((2, 2, 8, edge), F32),
            pltpu.VMEM((2, 2, 2 * nz, 8, edge), F32),
            pltpu.SemaphoreType.DMA((2,)),
            pltpu.SemaphoreType.DMA((n_copies,)),
            pltpu.SemaphoreType.DMA((n_copies,)),
        ],
        compiler_params=pltpu.CompilerParams(
            collective_id=0, has_side_effects=True, vmem_limit_bytes=56 * 1024 * 1024
        ),
        cost_estimate=pl.CostEstimate(
            flops=8 * slots * edge**3, bytes_accessed=4 * 1024 * 1024, transcendentals=0
        ),
    )(rows, cols, count, values, right_side, penalties)


def solution(mesh):
    nz, nf = mesh.shape["comp"] // 2, mesh.shape["feat"]
    placed = (
        P("comp", "feat", None, None, None),
        P("comp", "feat", None),
        P("comp", "feat", None),
        P("comp", "feat"),
        P(("comp", "feat"), None),
        P(),
    )
    return jax.shard_map(
        functools.partial(shards, nz, nf),
        mesh=mesh,
        in_specs=placed,
        out_specs=(P("feat", None), P(("comp", "feat"), None)),
        check_vma=False,
    )
```

```python
import functools

import jax
import jax.numpy as jnp
from jax import lax
from jax.experimental import pallas as pl
from jax.experimental.pallas import tpu as pltpu
from jax.sharding import PartitionSpec as P

CB_DEV = 14
MESH = pl.DeviceIdType.MESH
F32 = jnp.float32
BF16 = jnp.bfloat16


def fold(x):
    return x + pltpu.roll(x, x.shape[1] // 2, axis=1)


def kernel(
    nz, nf, slots, rb, edge, sr,
    rows, cols, count, values_in, rs_in, ridge, sol_out, res_out,
    values, rs, vt, run_a, run_b, panel_a, panel_b, chosen_a, chosen_b, product_a, product_b, slabs, part, sib, pair, zbuf, dirs, img, rbuf,
    r_f32, g_f32, i_f32, link, sc_src, sc_feat, sc_mid, sc_comp, load_sems, send_sems, recv_sems,
):
    comp, feat = lax.axis_index("comp"), lax.axis_index("feat")
    core, z = lax.rem(comp, 2), comp // 2
    low = edge // 2
    half = CB_DEV // 2 * low
    hp = nz * sr
    own_blocks = rb // nf
    sibling = {"comp": comp + 1 - 2 * core}
    n_comp = 2 * nz
    pending = []
    used = [0]
    mine = pl.ds(feat * own_blocks, own_blocks)

    def zpeer(k):
        return {"comp": lax.rem(z + k, nz) * 2 + core}

    def fpeer(k):
        return {"feat": lax.rem(feat + k, nf)}

    def cpeer(k):
        return {"comp": lax.rem(comp + k, n_comp)}

    def send(src, dst, device):
        at = used[0]
        used[0] += 1
        copy = pltpu.make_async_remote_copy(
            src_ref=src,
            dst_ref=dst,
            send_sem=send_sems.at[at],
            recv_sem=recv_sems.at[at],
            device_id=device,
            device_id_type=MESH,
        )
        copy.start()
        pending.append(copy)
        return copy

    def shard(k):
        return pl.multiple_of(lax.rem(z + k, nz) * sr, 16)

    prev_c, last_c = 0, slots
    prev_r, last_r = slots + CB_DEV, 2 * slots + CB_DEV

    def make_links(keys, groups, prev, last):
        seen = [jnp.int32(slots) for _ in range(groups)]
        live = count[0]
        for s in range(slots):
            key = keys[s]
            before = jnp.int32(slots)
            for q in range(groups):
                before = jnp.where(key == q, seen[q], before)
            link[prev + s] = before
            key = jnp.where(s < live, key, -1)
            for q in range(groups):
                seen[q] = jnp.where(key == q, s, seen[q])
        for q in range(groups):
            link[last + q] = seen[q]

    left = lax.broadcasted_iota(jnp.int32, (low, edge), 1) < low

    def swap(x):
        return pltpu.roll(x, low, axis=1)

    def widen(packed):
        x = packed.astype(F32)
        y = swap(x)
        zero = jnp.zeros_like(x)
        return jnp.concatenate(
            [
                jnp.where(left, x, zero).astype(BF16),
                jnp.where(left, y, zero).astype(BF16),
                jnp.where(left, zero, y).astype(BF16),
                jnp.where(left, zero, x).astype(BF16),
            ],
            axis=0,
        )

    def unpack(x0, x1):
        return jnp.where(left, x0, swap(x1)), jnp.where(left, swap(x0), x1)

    def column_sum(x):
        return jnp.sum(x, axis=0, keepdims=True)

    def stream(h):
        run = (run_a, run_b)[h]
        panel = (panel_a, panel_b)[h]
        chosen = (chosen_a, chosen_b)[h]
        product = (product_a, product_b)[h]

        def gather_feat(it):
            at = (it, h, mine)
            return [send(slabs.at[at], slabs.at[at], fpeer(k)) for k in range(1, nf)]

        def products(blocks, places, prev):
            for s in range(slots):
                chosen[s] = panel[places[s]]
            for s in range(slots):
                block = jnp.concatenate([blocks[s, :low], blocks[s, low:]], axis=1)
                product[s] = jnp.dot(block, widen(chosen[s]), preferred_element_type=F32)
            for s in range(slots):
                run[s] = product[s] + run[link[prev + s]]

        def backward(it):
            for r in range(rb):
                panel[r] = slabs[it, h, r]
            products(vt, rows, prev_c)
            for q in range(CB_DEV):
                d, p = q // (CB_DEV // 2), q % (CB_DEV // 2)
                part[it, h, pl.ds(d * hp + p * low, low)] = run[link[last_c + q]]
            if hp > half:
                for d in range(2):
                    part[it, h, pl.ds(d * hp + half, hp - half)] = jnp.zeros((hp - half, edge), F32)

        def scatter_comp(it):
            order = list(range(1, nz)) + [0]
            theirs = pl.multiple_of((1 - core) * hp, 16)
            whole = send(part.at[it, h, pl.ds(theirs, hp)], sib.at[it, h], sibling)
            yield
            arrivals = []
            total = None
            whole.wait_recv()
            for k in order:
                ours = pl.multiple_of(core * hp + shard(k), 16)
                both = part[it, h, pl.ds(ours, sr)] + sib[it, h, pl.ds(shard(k), sr)]
                if k:
                    pair[it, h, k] = both.astype(BF16)
                    arrivals.append(send(pair.at[it, h, k], zbuf.at[it, h, k], zpeer(k)))
                else:
                    total = both
            yield
            for k, copy in zip(order, arrivals):
                copy.wait_recv()
                total = total + zbuf[it, h, k].astype(F32)
            return total

        def gather_comp(it, piece):
            here = (it, h, pl.ds(pl.multiple_of(core * hp + shard(0), 16), sr))
            dirs[here] = piece.astype(BF16)
            across = [send(dirs.at[here], dirs.at[here], zpeer(k)) for k in range(1, nz)]
            yield
            for copy in across:
                copy.wait_recv()
            ours = (it, h, pl.ds(pl.multiple_of(core * hp, 16), hp))
            beside = send(dirs.at[ours], dirs.at[ours], sibling)
            yield
            beside.wait_recv()

        def forward(it):
            for q in range(CB_DEV):
                d, p = q // (CB_DEV // 2), q % (CB_DEV // 2)
                panel[q] = dirs[it, h, pl.ds(d * hp + p * low, low)]
            products(values, cols, prev_r)
            for r in range(rb):
                img[it, h, r] = run[link[last_r + r]].astype(BF16)

        def scatter_feat(it):
            copies = [
                send(
                    img.at[it, h, pl.ds(lax.rem(feat + k, nf) * own_blocks, own_blocks)],
                    rbuf.at[it, h, k],
                    fpeer(k),
                )
                for k in range(1, nf)
            ]
            yield
            total = img[it, h, mine].astype(F32)
            for k, copy in zip(range(1, nf), copies):
                copy.wait_recv()
                total = total + rbuf[it, h, k].astype(F32)
            return total.reshape(own_blocks * low, edge)

        def sums(it, parts):
            for i, row in enumerate(parts):
                sc_src[it, h, pl.ds(i, 1)] = row
            copies = [
                send(sc_src.at[it, h], sc_feat.at[it, h, k], fpeer(k)) for k in range(1, nf)
            ]
            yield
            total = sc_src[it, h]
            for k, copy in zip(range(1, nf), copies):
                copy.wait_recv()
                total = total + sc_feat[it, h, k]
            sc_mid[it, h] = total
            copies = [
                send(sc_mid.at[it, h], sc_comp.at[it, h, k], cpeer(k)) for k in range(1, n_comp)
            ]
            yield
            for k, copy in zip(range(1, n_comp), copies):
                copy.wait_recv()
                total = total + sc_comp[it, h, k]
            return fold(total)

        copies = gather_feat(0)
        yield
        for copy in copies:
            copy.wait_recv()
        backward(0)
        g0 = yield from scatter_comp(0)
        g_f32[h] = g0
        yield from gather_comp(0, g0)
        forward(0)
        i0 = yield from scatter_feat(0)
        i_f32[h] = i0
        g0 = g_f32[h]
        first = yield from sums(0, [column_sum(i0 * i0), column_sum(g0 * g0)])
        every = jnp.broadcast_to(ridge[...], (8, edge))
        here, there = (every, swap(every)) if h == 0 else (swap(every), every)
        penalty = jnp.where(left[:8], here, there)[0:1]
        image0, energy0 = first[0:1], first[1:2]
        step0 = energy0 / (image0 + penalty * energy0)
        r1 = r_f32[h] - step0 * i_f32[h]
        slabs[1, h, mine] = r1.astype(BF16).reshape(own_blocks, low, edge)
        copies = gather_feat(1)
        yield
        for copy in copies:
            copy.wait_recv()
        backward(1)
        g1 = yield from scatter_comp(1)
        g0 = g_f32[h]
        g1 = g1 - penalty * (step0 * g0)
        energy_row, mixed_row = column_sum(g1 * g1), column_sum(g1 * g0)
        yield from gather_comp(1, g1)
        forward(1)
        u = yield from scatter_feat(1)
        i0 = i_f32[h]
        last = yield from sums(
            1, [column_sum(u * u), column_sum(u * i0), energy_row, mixed_row]
        )
        uu, ui, energy1, gg = last[0:1], last[1:2], last[2:3], last[3:4]
        beta = energy1 / energy0
        curvature = (
            uu + beta * (2.0 * ui + beta * image0)
            + penalty * (energy1 + beta * (2.0 * gg + beta * energy0))
        )
        step1 = energy1 / curvature
        weight = step0 + step1 * beta
        r_f32[h] = r_f32[h] - weight * i_f32[h] - step1 * u
        return weight, step1

    load_rs = pltpu.make_async_copy(rs_in, rs, load_sems.at[0])
    load_rs.start()
    load_values = pltpu.make_async_copy(values_in, values, load_sems.at[1])
    load_values.start()
    barrier = pltpu.get_barrier_semaphore()
    for k in range(1, n_comp):
        pl.semaphore_signal(barrier, inc=1, device_id=cpeer(k), device_id_type=MESH)
    for k in range(1, nf):
        pl.semaphore_signal(barrier, inc=1, device_id=fpeer(k), device_id_type=MESH)
    sc_src[...] = jnp.zeros_like(sc_src)
    load_rs.wait()
    for r in range(own_blocks):
        top, bottom = rs[pl.ds(r * edge, low)], rs[pl.ds(r * edge + low, low)]
        for h, x in enumerate(unpack(top, bottom)):
            r_f32[h, pl.ds(r * low, low)] = x
    for h in range(2):
        slabs[0, h, mine] = r_f32[h].astype(BF16).reshape(own_blocks, low, edge)
    pl.semaphore_wait(barrier, n_comp - 1 + nf - 1)

    streams = [stream(h) for h in range(2)]
    steps = [None, None]
    next(streams[0])
    run_a[slots] = jnp.zeros((low, edge), F32)
    run_b[slots] = jnp.zeros((low, edge), F32)
    make_links(cols, CB_DEV, prev_c, last_c)
    make_links(rows, rb, prev_r, last_r)
    load_values.wait()
    for s in range(slots):
        vt[s] = values[s].T
    next(streams[0])
    turns, done_sends = [0], 0
    while None in steps:
        for h, g in reversed(list(enumerate(streams))):
            if steps[h] is not None:
                continue
            turns.append(len(pending))
            while done_sends < turns[max(len(turns) - 4, 0)]:
                pending[done_sends].wait_send()
                done_sends += 1
            try:
                next(g)
            except StopIteration as done:
                steps[h] = done.value
    for r in range(own_blocks):
        parts = unpack(r_f32[0, pl.ds(r * low, low)], r_f32[1, pl.ds(r * low, low)])
        for d in range(2):
            res_out[pl.ds(r * edge + d * low, low)] = parts[d]
    for q in range(CB_DEV):
        d, p = q // (CB_DEV // 2), q % (CB_DEV // 2)
        take = pl.ds(d * hp + p * low, low)
        found = [
            steps[h][0] * dirs[0, h, take].astype(F32) + steps[h][1] * dirs[1, h, take].astype(F32)
            for h in range(2)
        ]
        parts = unpack(*found)
        for d in range(2):
            sol_out[pl.ds(q * edge + d * low, low)] = parts[d]
    for copy in pending[done_sends:]:
        copy.wait_send()


def shards(nz, nf, block_values, block_rows, block_cols, block_counts, right_side, ridge):
    values = block_values[0, 0]
    rows, cols, count = block_rows[0, 0], block_cols[0, 0], block_counts[0]
    slots, edge = values.shape[0], values.shape[1]
    held = right_side.shape[0]
    rb = held * nf // edge
    low = edge // 2
    sr = -(-(CB_DEV // 2 * low) // (nz * 16)) * 16
    hp = nz * sr
    own = rb // nf
    n_copies = 4 * (2 * (nf - 1) + 2 * (nz - 1) + 2 + (nf - 1) + (2 * nz - 1))
    smem = pl.BlockSpec(memory_space=pltpu.SMEM)
    anywhere = pl.BlockSpec(memory_space=pltpu.HBM)
    vmem = pl.BlockSpec(memory_space=pltpu.VMEM)
    return pl.pallas_call(
        functools.partial(kernel, nz, nf, slots, rb, edge, sr),
        out_shape=(
            jax.ShapeDtypeStruct((CB_DEV * edge, edge), F32),
            jax.ShapeDtypeStruct((held, edge), F32),
        ),
        in_specs=[smem, smem, smem, anywhere, anywhere, vmem],
        out_specs=(vmem, vmem),
        scratch_shapes=[
            pltpu.VMEM((slots, edge, edge), BF16),
            pltpu.VMEM((held, edge), F32),
            pltpu.VMEM((slots, edge, edge), BF16),
            pltpu.VMEM((slots + 1, low, edge), F32),
            pltpu.VMEM((slots + 1, low, edge), F32),
            pltpu.VMEM((max(rb, CB_DEV), low, edge), BF16),
            pltpu.VMEM((max(rb, CB_DEV), low, edge), BF16),
            pltpu.VMEM((slots, low, edge), BF16),
            pltpu.VMEM((slots, low, edge), BF16),
            pltpu.VMEM((slots, low, edge), F32),
            pltpu.VMEM((slots, low, edge), F32),
            pltpu.VMEM((2, 2, rb, low, edge), BF16),
            pltpu.VMEM((2, 2, 2 * hp, edge), F32),
            pltpu.VMEM((2, 2, hp, edge), F32),
            pltpu.VMEM((2, 2, nz, sr, edge), BF16),
            pltpu.VMEM((2, 2, nz, sr, edge), BF16),
            pltpu.VMEM((2, 2, 2 * hp, edge), BF16),
            pltpu.VMEM((2, 2, rb, low, edge), BF16),
            pltpu.VMEM((2, 2, nf, own, low, edge), BF16),
            pltpu.VMEM((2, own * low, edge), F32),
            pltpu.VMEM((2, sr, edge), F32),
            pltpu.VMEM((2, own * low, edge), F32),
            pltpu.SMEM((2 * slots + CB_DEV + rb,), jnp.int32),
            pltpu.VMEM((2, 2, 8, edge), F32),
            pltpu.VMEM((2, 2, nf, 8, edge), F32),
            pltpu.VMEM((2, 2, 8, edge), F32),
            pltpu.VMEM((2, 2, 2 * nz, 8, edge), F32),
            pltpu.SemaphoreType.DMA((2,)),
            pltpu.SemaphoreType.DMA((n_copies,)),
            pltpu.SemaphoreType.DMA((n_copies,)),
        ],
        compiler_params=pltpu.CompilerParams(
            collective_id=0, has_side_effects=True, vmem_limit_bytes=48 * 1024 * 1024
        ),
        cost_estimate=pl.CostEstimate(
            flops=8 * slots * edge**3, bytes_accessed=4 * 1024 * 1024, transcendentals=0
        ),
    )(rows, cols, count, values, right_side, ridge.reshape(1, edge))


def solution(mesh):
    nz, nf = mesh.shape["comp"] // 2, mesh.shape["feat"]
    placed = (
        P("comp", "feat", None, None, None),
        P("comp", "feat", None),
        P("comp", "feat", None),
        P("comp", "feat"),
        P(("comp", "feat"), None),
        P(),
    )
    return jax.shard_map(
        functools.partial(shards, nz, nf),
        mesh=mesh,
        in_specs=placed,
        out_specs=(P("feat", None), P(("comp", "feat"), None)),
        check_vma=False,
    )
```
